1024 devices in a mesh: dp: 16 (over y, z_hi), seq: 8 (over z_lo), expert: 8 (over x, core).
Axes of the slice: x: 4, y: 4, z: 32 (z_hi: 4, z_lo: 8; z = z_hi * 8 + z_lo), core: 2. Of those that a mesh axis runs over, the one named last changes fastest.
Arguments:
- acts: bfloat16 [16384, 3072], P(('dp', 'seq')), parts along dimension 0, may hold values from -6 to 6
- tangents: bfloat16 [16384, 3072], P(('dp', 'seq')), parts along dimension 0, may hold values from -6 to 6
- cotangents: bfloat16 [16384, 3072], P(('dp', 'seq')), parts along dimension 0, may hold values from -6 to 6
- routes: int32 [16384, 2], P(('dp', 'seq')), parts along dimension 0, may hold values from 0 to 7, all different within a row; in each aligned block of 128 rows (0 to 127, 128 to 255, ...) at most 34 rows name the same one
- gates: float32 [16384, 2], P(('dp', 'seq')), parts along dimension 0, may hold values from 0.1 to 1
- w_in: bfloat16 [8, 3072, 4096], P('expert', None, 'seq'), may hold values from -0.109375 to 0.109375
- w_out: bfloat16 [8, 4096, 3072], P('expert', 'seq'), may hold values from -0.09375 to 0.09375
Outputs:
- tan_out: bfloat16 [16384, 3072], P(('dp', 'seq'), 'expert'), parts along dimension 0
- grad_in: bfloat16 [16384, 3072], P(('dp', 'seq'), 'expert'), parts along dimension 0
The draws below stay inside these ranges and needn't reach their ends.
There are 16 independent parts, one for each index of `dp`. The reference program is written for one: setup_inputs(seed, part) draws one part's arguments, and reference() takes and returns one part's arrays. A program takes and returns all parts, laid end to end along the dimension named above; an argument that names none is the same for every part. Nothing has to cross between parts.
Inputs may be any that keep to these rules, and one draw needn't show every extreme that they name: `routes`: each row names two different experts; in each aligned block of 128 rows (the rows of one index of seq) no expert is named by more than 34 rows, and some expert reaches 34 in some block.
All inputs are finite; a program needn't handle non-finite values.
Results may differ from the reference program's by a relative error of at most 0.02.
Values may be sent and summed in bfloat16 or wider, within the bound.
A program may use at most 64 MiB of HBM per device.

```python
import math
import jax
import jax.numpy as jnp
import numpy as np
from jax import lax

D = 3072
FF = 4096
ROWS = 128
EXPERTS = 8
CAP = 34
TOKENS = 1024
N_SEQ = 8


def shard_levels(stream_key, extent, pieces, least, high):
    level = 1.0
    for axis_at, parts in pieces:
        draws = jax.random.uniform(jax.random.fold_in(jax.random.fold_in(stream_key, 6), axis_at), (parts,), jnp.float32, least / len(pieces), high / len(pieces))
        level = level * jnp.repeat(jnp.exp(draws), extent[axis_at] // parts).reshape((-1,) + (1,) * (len(extent) - 1 - axis_at))
    return level


def assign_block(rng, own, number, rows, count, top, limit, slope):
    ranking = jax.random.permutation(rng, count)
    packed, common = portions_of(count, rows * top, limit, slope, True), portions_of(count, rows * top, limit, slope, False)
    places = jnp.arange(count)

    def named(lengths, offset_by):
        used = int((lengths > 0).sum())
        fixed = max(1, used // 4)
        passed = fixed + (places - fixed + offset_by * (used - fixed)) % max(1, count - fixed)
        return jnp.zeros((count,), jnp.int32).at[ranking[jnp.where(places < fixed, places, passed)]].set(jnp.asarray(lengths, jnp.int32))

    lengths = jnp.where(number % 4 == 0, named(packed, number // 4), named(common, number - number // 4 - 1))
    mixed = jax.random.permutation(jax.random.fold_in(own, 3), count)
    giver, receiver = mixed[0:count // 2 * 2:2], mixed[1:count // 2 * 2:2]
    slack = jnp.minimum(lengths[giver] - 1, limit - lengths[receiver]) // 2
    slack = jnp.where((giver == ranking[0]) | (receiver == ranking[0]) | (lengths[receiver] == 0), 0, jnp.maximum(slack, 0))
    passed = jax.random.randint(jax.random.fold_in(own, 4), (count // 2,), 0, 1 << 20) % (slack + 1)
    lengths = lengths.at[giver].add(-passed).at[receiver].add(passed)
    items = jnp.searchsorted(jnp.cumsum(lengths), jnp.arange(rows * top), side="right").astype(jnp.int32)
    listing = items.reshape(top, rows).T
    listing = listing[jax.random.permutation(jax.random.fold_in(own, 1), rows)]
    offset_by = jax.random.randint(jax.random.fold_in(own, 2), (rows, 1), 0, top)
    return jnp.take_along_axis(listing, (jnp.arange(top)[None, :] + offset_by) % top, axis=1)


def portions_of(count, total, bound, skew, full):
    portions = [(1 << 20) // math.isqrt(standing ** skew) + 1 for standing in range(1, count + 1)]
    largest = bound if full else min(bound, max(-(-total // count), total * portions[0] // sum(portions)))
    least = 1 if total - largest >= count - 1 else 0
    counts, spare = [largest] + [least] * (count - 1), total - largest - least * (count - 1)
    while spare > 0:
        free = [i for i in range(1, count) if counts[i] < largest] or [i for i in range(1, count) if counts[i] < bound]
        whole, remaining = sum([portions[i] for i in free]), spare
        for i in free:
            extra = min(bound - counts[i], max(1, remaining * portions[i] // whole), spare)
            counts[i] = counts[i] + extra
            spare = spare - extra
    return np.array(counts)


def gaussian(stream_key, dims, scale, most, split=(), held_as=jnp.bfloat16):
    factor_of = shard_levels(stream_key, dims, split, -0.22, 0.18) if split else 1.0
    entries = jax.random.normal(stream_key, dims, jnp.float32) * scale * factor_of
    return jnp.minimum(jnp.maximum(entries, -most), most).astype(held_as)


def setup_inputs(seed: int = 0, part: int = 0) -> dict:
    splits = jax.random.split(jax.random.key(seed), 8)
    own_keys = jax.random.split(jax.random.fold_in(splits[7], part), 8)
    acts = gaussian(own_keys[0], (TOKENS, D), 1.0, 6.0, ((0, 8),))
    tangents = gaussian(own_keys[1], (TOKENS, D), 1.0, 6.0, ((0, 8),))
    cotangents = gaussian(own_keys[2], (TOKENS, D), 1.0, 6.0, ((0, 8),))
    routes_keys = jax.random.split(jax.random.fold_in(own_keys[3], 1), TOKENS // ROWS)
    routes_turns = jax.random.permutation(jax.random.fold_in(own_keys[3], 3), TOKENS // ROWS)
    routes = jax.vmap(lambda own, number: assign_block(jax.random.fold_in(own_keys[3], 2), own, number, ROWS, EXPERTS, 2, CAP, 1))(routes_keys, routes_turns).reshape((TOKENS, 2))
    gates = jnp.clip(jnp.exp(math.log(1.0) - 2.3025851 * jax.random.uniform(own_keys[4], (TOKENS, 2), jnp.float32) ** shard_levels(own_keys[4], (TOKENS, 2), ((0, 8),), -0.2, 0.2)), 0.1, 1.0)
    w_in = gaussian(splits[5], (EXPERTS, D, FF), D ** -0.5, 0.109375, ((0, 8), (2, 8)))
    w_out = gaussian(splits[6], (EXPERTS, FF, D), FF ** -0.5, 0.09375, ((0, 8), (1, 8)))
    return {"acts": acts, "tangents": tangents, "cotangents": cotangents, "routes": routes, "gates": gates, "w_in": w_in, "w_out": w_out}


def round_keep(value):
    low = lax.optimization_barrier(value.astype(jnp.bfloat16))
    return low.astype(jnp.float32)


def expert_values(expert_id, acts, tangents, cotangents, routes, gates, w_in, w_out):
    routed = jnp.any(routes == expert_id, axis=1)
    order = jnp.argsort(jnp.where(routed, 0, 1).astype(jnp.int32), stable=True)
    chosen = order[: N_SEQ * CAP].astype(jnp.int32)
    rows_x = acts[chosen]
    rows_t = tangents[chosen]
    rows_c = cotangents[chosen]
    w_first = w_in[expert_id]
    w_second = w_out[expert_id]
    block = FF // N_SEQ
    acc_tan = jnp.zeros((N_SEQ * CAP, D), jnp.float32)
    acc_grad = jnp.zeros((N_SEQ * CAP, D), jnp.float32)
    for index in range(N_SEQ):
        w_one = w_first[:, index * block:(index + 1) * block]
        w_two = w_second[index * block:(index + 1) * block, :]
        hidden = jnp.dot(rows_x, w_one, preferred_element_type=jnp.float32)
        moved = jnp.dot(rows_t, w_one, preferred_element_type=jnp.float32)
        back = jnp.dot(rows_c, w_two.T, preferred_element_type=jnp.float32)
        sig = jax.nn.sigmoid(hidden)
        first = (sig * (1.0 + hidden * (1.0 - sig)) * moved).astype(jnp.bfloat16)
        second = (sig * (1.0 - sig) * (2.0 + hidden * (1.0 - 2.0 * sig)) * moved * back).astype(jnp.bfloat16)
        acc_tan = acc_tan + round_keep(jnp.dot(first, w_two, preferred_element_type=jnp.float32))
        acc_grad = acc_grad + round_keep(jnp.dot(second, w_one.T, preferred_element_type=jnp.float32))
    weight = jnp.sum(jnp.where(routes[chosen] == expert_id, gates[chosen], 0.0), axis=1)
    return chosen, weight, round_keep(acc_tan), round_keep(acc_grad)


def reference(acts, tangents, cotangents, routes, gates, w_in, w_out):
    total_tan = jnp.zeros((TOKENS, D), jnp.float32)
    total_grad = jnp.zeros((TOKENS, D), jnp.float32)
    for expert_id in range(EXPERTS):
        chosen, weight, slot_tan, slot_grad = expert_values(expert_id, acts, tangents, cotangents, routes, gates, w_in, w_out)
        total_tan = total_tan.at[chosen].add(weight[:, None] * slot_tan)
        total_grad = total_grad.at[chosen].add(weight[:, None] * slot_grad)
    return total_tan.astype(jnp.bfloat16), total_grad.astype(jnp.bfloat16)
```

```python
import functools

import jax
import jax.numpy as jnp
from jax import lax
from jax.experimental import pallas as pl
from jax.experimental.pallas import tpu as pltpu
from jax.sharding import PartitionSpec as P

MESH = pl.DeviceIdType.MESH
E = 8
N = 8
CAP = 34
MAIN = 32
Z_RUNS = 4
POS = {0: 0, 1: 1, 2: 2, 5: 3, 6: 4, 3: 5, 7: 6, 4: 7}
EARLY = 5


def dot(a, b, dims=((1,), (0,))):
    return lax.dot_general(a, b, (dims, ((), ())), preferred_element_type=jnp.float32)


NT = ((1,), (1,))
TN = ((0,), (0,))


def kernel(
    runs, routes_ref, gates_ref, acts_ref, tangents_ref, cotangents_ref, w_in_hbm, w_out_hbm,
    tan_ref, grad_ref,
    w_in, w_out, rows, extra, mid, part, part_extra, back, back_extra, slots, final,
    w_sems, gather_send, gather_recv, reduce_send, reduce_recv, swap_send, swap_recv,
):
    dp = lax.axis_index("dp")
    seq = lax.axis_index("seq")
    me = lax.axis_index("expert")
    width = acts_ref.shape[1]
    piece = width // E
    toks = acts_ref.shape[0]
    bf16, f32 = jnp.bfloat16, jnp.float32

    load_in = pltpu.make_async_copy(w_in_hbm.at[0], w_in, w_sems.at[0])
    load_out = pltpu.make_async_copy(w_out_hbm.at[0], w_out, w_sems.at[1])
    load_in.start()
    load_out.start()

    ring = runs * N
    place = (dp % runs) * N + seq
    column = dp - dp % runs
    step = 1 - 2 * (me % 2)

    def at(offset):
        there = (place + offset * step + ring) % ring
        return (column + there // N, there % N, me)

    ahead, behind = at(1), at(-1)
    others = [(dp, seq, (me + i) % E) for i in range(1, E)]

    barrier = pltpu.get_barrier_semaphore()
    for device in [ahead, behind] + others:
        pl.semaphore_signal(barrier, inc=1, device_id=device, device_id_type=MESH)

    routes = routes_ref[...]
    experts = lax.broadcasted_iota(jnp.int32, (E, toks), 0)
    first_hit = routes[0:1, :] == experts
    second_hit = routes[1:2, :] == experts
    named = jnp.where(first_hit | second_hit, 1.0, 0.0)
    earlier = jnp.where(
        lax.broadcasted_iota(jnp.int32, (toks, toks), 0) < lax.broadcasted_iota(jnp.int32, (toks, toks), 1), 1.0, 0.0
    ).astype(bf16)
    count = dot(named.astype(bf16), earlier)
    slot_all = jnp.where(named > 0.5, count, -1.0).astype(jnp.int32)
    own_row = experts == me
    slot = jnp.sum(jnp.where(own_row, slot_all, 0), axis=0, keepdims=True)
    gate = jnp.sum(
        jnp.where(own_row & first_hit, gates_ref[0:1, :], 0.0)
        + jnp.where(own_row & second_hit, gates_ref[1:2, :], 0.0),
        axis=0, keepdims=True,
    )
    hits = lax.broadcasted_iota(jnp.int32, (48, toks), 0) == slot
    pick = jnp.where(hits[0:MAIN], 1.0, 0.0).astype(bf16)
    slot_gate = jnp.sum(jnp.where(hits, gate, 0.0), axis=1, keepdims=True)
    pack_row = lax.broadcasted_iota(jnp.int32, (16, toks), 0)
    pack_hit = jnp.where(slot == MAIN + pack_row % 2, 1.0, 0.0)

    sources = (acts_ref, tangents_ref, cotangents_ref)
    for a, source in enumerate(sources):
        rows[a, 0:MAIN, :] = dot(pick, source[...]).astype(bf16)
        packed = jnp.zeros((16, piece), f32)
        for j in range(E):
            chosen = jnp.where(pack_row // 2 == j, pack_hit, 0.0).astype(bf16)
            packed = packed + dot(chosen, source[:, j * piece:(j + 1) * piece])
        extra[0:16, a * piece:(a + 1) * piece] = packed.astype(bf16)

    pl.semaphore_wait(barrier, len(others) + 2)

    def main_rows(k):
        return pl.ds(POS[k] * MAIN, MAIN)

    def gather_copy(k_from, k_to, c, device):
        if c < 3:
            src, dst = rows.at[c, main_rows(k_from), :], rows.at[c, main_rows(k_to), :]
        else:
            src, dst = extra.at[pl.ds(16 * k_from, 16), :], extra.at[pl.ds(16 * k_to, 16), :]
        return pltpu.make_async_remote_copy(
            src_ref=src, dst_ref=dst, send_sem=gather_send.at[k_to, c], recv_sem=gather_recv.at[k_to, c],
            device_id=device, device_id_type=MESH,
        )

    sent = []

    def forward(k_from, k_to, c, device):
        copy = gather_copy(k_from, k_to, c, device)
        copy.start()
        sent.append(copy)

    parts = (3, 0, 1, 2)

    def arrived(k, c):
        gather_copy(k, k, c, ahead).wait_recv()

    for c in parts:
        forward(0, 1, c, ahead)
        forward(0, 5, c, behind)
    for hop in (1, 2):
        for c in parts:
            arrived(hop, c)
            forward(hop, hop + 1, c, ahead)
            arrived(hop + 4, c)
            forward(hop + 4, hop + 5, c, behind)

    def compute(start, size):
        def hidden_tile(i, carry):
            f = pl.ds(pl.multiple_of(i * 256, 256), 256)
            both = dot(rows[0:2, start:start + size, :].reshape(2 * size, width), w_in[:, f])
            h, u = both[0:size], both[size:2 * size]
            p = dot(rows[2, start:start + size, :], w_out[f, :], NT)
            s = jax.nn.sigmoid(h)
            mid[0, start:start + size, f] = (s * (1.0 + h * (1.0 - s)) * u).astype(bf16)
            mid[1, start:start + size, f] = (
                s * (1.0 - s) * (2.0 + h * (1.0 - 2.0 * s)) * u * p
            ).astype(bf16)
            return carry

        lax.fori_loop(0, w_in.shape[1] // 256, hidden_tile, 0)

        def out_tile(i, carry):
            d = pl.ds(pl.multiple_of(i * 256, 256), 256)
            part[0, start:start + size, d] = dot(mid[0, start:start + size, :], w_out[:, d]).astype(bf16)
            part[1, start:start + size, d] = dot(mid[1, start:start + size, :], w_in[d, :], NT).astype(bf16)
            return carry

        lax.fori_loop(0, width // 256, out_tile, 0)

    load_in.wait()
    load_out.wait()
    compute(0, EARLY * MAIN)
    for c in parts:
        arrived(3, c)
        forward(3, 4, c, ahead)
    for c in parts:
        arrived(7, c)
    arrived(4, 3)

    at_row = lax.broadcasted_iota(jnp.int32, (128, 128), 0)
    at_col = lax.broadcasted_iota(jnp.int32, (128, 128), 1)
    turn = (at_row // 16) == (at_col % 16) // 2
    turn = turn & ((at_row % 16) // 2 == at_col // 16) & (at_row % 2 == at_col % 2)
    turn = jnp.where(turn, 1.0, 0.0).astype(bf16)
    late = N * MAIN
    for a in range(3):
        turned = dot(turn, extra[:, a * piece:(a + 1) * piece]).astype(bf16)
        for j in range(E):
            rows[a, late:late + 16, j * piece:(j + 1) * piece] = turned[j * 16:(j + 1) * 16]
    for c in (0, 1, 2):
        arrived(4, c)
    compute(EARLY * MAIN, (N - EARLY) * MAIN + 16)

    for a in range(2):
        spread = jnp.concatenate(
            [part[a, late:late + 16, j * piece:(j + 1) * piece] for j in range(E)], axis=0
        )
        part_extra[:, a * piece:(a + 1) * piece] = dot(turn, spread).astype(bf16)

    def landing(k_from):
        return {4: 3, 3: 2, 2: 1, 1: 0, 7: 5, 6: 4, 5: 6}[k_from]

    def reduce_copy(k_from, c, device):
        slot_at = landing(k_from)
        if c < 2:
            src, dst = part.at[c, main_rows(k_from), :], back.at[slot_at, c]
        else:
            src, dst = part_extra.at[pl.ds(16 * k_from, 16), :], back_extra.at[slot_at]
        return pltpu.make_async_remote_copy(
            src_ref=src, dst_ref=dst, send_sem=reduce_send.at[slot_at, c], recv_sem=reduce_recv.at[slot_at, c],
            device_id=device, device_id_type=MESH,
        )

    def give(k, c, device):
        copy = reduce_copy(k, c, device)
        copy.start()
        sent.append(copy)

    def add(k, k_from, c):
        slot_at = landing(k_from)
        reduce_copy(k_from, c, ahead).wait_recv()
        if c < 2:
            r = main_rows(k)
            part[c, r, :] = (part[c, r, :].astype(f32) + back[slot_at, c].astype(f32)).astype(bf16)
        else:
            r = pl.ds(16 * k, 16)
            part_extra[r, :] = (part_extra[r, :].astype(f32) + back_extra[slot_at].astype(f32)).astype(bf16)

    order = (0, 1, 2)
    for c in order:
        give(4, c, behind)
        give(7, c, ahead)
    for c in order:
        add(3, 4, c)
        give(3, c, behind)
        add(6, 7, c)
        give(6, c, ahead)
    for c in order:
        add(2, 3, c)
        give(2, c, behind)
        add(5, 6, c)
        give(5, c, ahead)
    for c in order:
        add(1, 2, c)
        give(1, c, behind)

    pick_row = lax.broadcasted_iota(jnp.int32, (16, 16), 0)
    pick_col = lax.broadcasted_iota(jnp.int32, (16, 16), 1)
    for c in order:
        reduce_copy(5, c, ahead).wait_recv()
        reduce_copy(1, c, ahead).wait_recv()
        if c < 2:
            total = part[c, 0:MAIN, :].astype(f32) + back[landing(5), c].astype(f32) + back[landing(1), c].astype(f32)
            slots[c, 0:MAIN, :] = (total * slot_gate[0:MAIN]).astype(bf16)
        else:
            total = (
                part_extra[0:16, :].astype(f32)
                + back_extra[landing(5)].astype(f32)
                + back_extra[landing(1)].astype(f32)
            ).astype(bf16)
            for j in range(E):
                select = jnp.where((pick_col == 2 * j + pick_row) & (pick_row < 2), 1.0, 0.0).astype(bf16)
                for a in range(2):
                    value = dot(select, total[:, a * piece:(a + 1) * piece]) * slot_gate[MAIN:48]
                    slots[a, MAIN:48, j * piece:(j + 1) * piece] = value.astype(bf16)

    swaps = []
    for i, device in enumerate(others):
        cols = pl.ds(pl.multiple_of(device[2] * piece, 128), piece)
        copy = pltpu.make_async_remote_copy(
            src_ref=slots.at[:, :, cols], dst_ref=final.at[i + 1],
            send_sem=swap_send.at[i], recv_sem=swap_recv.at[i], device_id=device, device_id_type=MESH,
        )
        copy.start()
        swaps.append(copy)
    final[0] = slots[:, :, pl.ds(pl.multiple_of(me * piece, 128), piece)]

    slot_axis = lax.broadcasted_iota(jnp.int32, (48, toks), 0)
    spreads = []
    for i in range(E):
        sender = (me - i + E) % E
        row = jnp.sum(jnp.where(experts == sender, slot_all, 0), axis=0, keepdims=True)
        spreads.append(jnp.where(slot_axis == row, 1.0, 0.0).astype(bf16))
    spread = jnp.concatenate(spreads, axis=0)
    for copy in swaps:
        copy.wait_recv()
    for a, out in enumerate((tan_ref, grad_ref)):
        out[...] = dot(spread, final[:, a].reshape(E * 48, piece), TN).astype(bf16)
    for copy in sent + swaps:
        copy.wait_send()


def solution(mesh):
    runs = Z_RUNS if mesh.shape["dp"] % Z_RUNS == 0 else 1

    def shards(acts, tangents, cotangents, routes, gates, w_in, w_out):
        toks, width = acts.shape
        hidden = w_in.shape[2]
        piece = width // E
        vmem = pl.BlockSpec(memory_space=pltpu.VMEM)
        hbm = pl.BlockSpec(memory_space=pl.ANY)
        bf16 = jnp.bfloat16
        total = N * MAIN + 16
        return pl.pallas_call(
            functools.partial(kernel, runs),
            out_shape=[jax.ShapeDtypeStruct((toks, piece), bf16)] * 2,
            in_specs=[vmem] * 5 + [hbm] * 2,
            out_specs=[vmem] * 2,
            scratch_shapes=[
                pltpu.VMEM((width, hidden), bf16),
                pltpu.VMEM((hidden, width), bf16),
                pltpu.VMEM((3, total, width), bf16),
                pltpu.VMEM((N * 16, 3 * piece), bf16),
                pltpu.VMEM((2, total, hidden), bf16),
                pltpu.VMEM((2, total, width), bf16),
                pltpu.VMEM((N * 16, 2 * piece), bf16),
                pltpu.VMEM((7, 2, MAIN, width), bf16),
                pltpu.VMEM((7, 16, 2 * piece), bf16),
                pltpu.VMEM((2, 48, width), bf16),
                pltpu.VMEM((E, 2, 48, piece), bf16),
                pltpu.SemaphoreType.DMA((2,)),
                pltpu.SemaphoreType.DMA((N, 4)),
                pltpu.SemaphoreType.DMA((N, 4)),
                pltpu.SemaphoreType.DMA((7, 3)),
                pltpu.SemaphoreType.DMA((7, 3)),
                pltpu.SemaphoreType.DMA((7,)),
                pltpu.SemaphoreType.DMA((7,)),
            ],
            compiler_params=pltpu.CompilerParams(
                collective_id=0, has_side_effects=True, vmem_limit_bytes=48 * 1024 * 1024
            ),
            cost_estimate=pl.CostEstimate(
                flops=10 * total * width * hidden, bytes_accessed=4 * width * hidden, transcendentals=total * hidden
            ),
        )(routes.T, gates.T, acts, tangents, cotangents, w_in, w_out)

    return jax.shard_map(
        shards,
        mesh=mesh,
        in_specs=(
            P(("dp", "seq"), None),
            P(("dp", "seq"), None),
            P(("dp", "seq"), None),
            P(("dp", "seq"), None),
            P(("dp", "seq"), None),
            P("expert", None, "seq"),
            P("expert", "seq", None),
        ),
        out_specs=(P(("dp", "seq"), "expert"), P(("dp", "seq"), "expert")),
        check_vma=False,
    )
```

```python
import functools

import jax
import jax.numpy as jnp
from jax import lax
from jax.experimental import pallas as pl
from jax.experimental.pallas import tpu as pltpu
from jax.sharding import PartitionSpec as P

MESH = pl.DeviceIdType.MESH
E = 8
N = 8
MAIN = 32
Z_RUNS = 4
POS = {0: 0, 1: 1, 2: 2, 5: 3, 6: 4, 3: 5, 7: 6, 4: 7}
EARLY = 5 * MAIN
EXTRA = N * MAIN
TOTAL = EXTRA + 16


def dot(a, b, dims=((1,), (0,))):
    return lax.dot_general(a, b, (dims, ((), ())), preferred_element_type=jnp.float32)


NT = ((1,), (1,))
TN = ((0,), (0,))


def main_rows(k):
    return pl.ds(POS[k] * MAIN, MAIN)


def block_of(side, d, i):
    if (side == 0) == (i % 2 == 0):
        return d
    return 4 + d if d <= 3 else None


def kernel(
    runs, routes_hbm, gates_hbm, acts_hbm, tangents_hbm, cotangents_hbm, w_in_hbm, w_out_hbm,
    tan_ref, grad_ref,
    routes_v, gates_v, acts_v, tangents_v, cotangents_v, w_in, w_out, raw_own, raw, metas, stage, tails, tails_out,
    rows, extra, gate_rows, mid, part, part_extra, back, back_extra, land, sums, sums_in, slots, final,
    load_sems, raw_send, raw_recv, meta_send, meta_recv, cot_send, cot_recv, pick_send, pick_recv,
    tail_send, tail_recv, land_send, land_recv, tan_send, tan_recv, sum_send, sum_recv, swap_send, swap_recv,
):
    dp = lax.axis_index("dp")
    seq = lax.axis_index("seq")
    me = lax.axis_index("expert")
    toks, width = acts_hbm.shape
    piece = width // E
    bf16, f32 = jnp.bfloat16, jnp.float32

    def cols(owner):
        return pl.ds(pl.multiple_of(owner * piece, 128), piece)

    loads = [
        pltpu.make_async_copy(src, dst, load_sems.at[n])
        for n, (src, dst) in enumerate((
            (acts_hbm.at[:, cols(me)], raw_own.at[0]),
            (tangents_hbm.at[:, cols(me)], raw_own.at[1]),
            (routes_hbm, routes_v),
            (gates_hbm, gates_v),
            (cotangents_hbm, cotangents_v),
            (acts_hbm, acts_v),
            (tangents_hbm, tangents_v),
            (w_in_hbm.at[0], w_in),
            (w_out_hbm.at[0], w_out),
        ))
    ]
    for load in loads:
        load.start()

    ring = runs * N
    place = (dp % runs) * N + seq
    column = dp - dp % runs
    step = 1 - 2 * (me % 2)

    def at(offset):
        there = (place + offset * step + ring) % ring
        return (column + there // N, there % N, me)

    ahead, behind = at(1), at(-1)
    away = (ahead, behind)
    home = (behind, ahead)
    others = [(dp, seq, (me + i) % E) for i in range(1, E)]

    barrier = pltpu.get_barrier_semaphore()
    for device in [ahead, behind] + others:
        pl.semaphore_signal(barrier, inc=1, device_id=device, device_id_type=MESH)

    sent = []

    def remote(src, dst, send, recv, device):
        return pltpu.make_async_remote_copy(
            src_ref=src, dst_ref=dst, send_sem=send, recv_sem=recv, device_id=device, device_id_type=MESH
        )

    def start(copy):
        copy.start()
        sent.append(copy)

    def raw_copy(side, d):
        src = raw_own if d == 1 else raw.at[side * 4 + d - 2]
        n = side * 4 + d - 1
        return remote(src, raw.at[n], raw_send.at[n], raw_recv.at[n], away[side])

    def meta_copy(side, d):
        n = side * 4 + d
        return remote(
            metas.at[0 if d == 1 else n - 1], metas.at[n], meta_send.at[n - 1], meta_recv.at[n - 1], away[side]
        )

    def cot_copies(side, d):
        k = side * 4 + d
        k_from = 0 if d == 1 else k - 1
        return [
            remote(
                rows.at[2, main_rows(k_from), :], rows.at[2, main_rows(k), :],
                cot_send.at[k, 0], cot_recv.at[k, 0], away[side],
            ),
            remote(
                extra.at[pl.ds(16 * k_from, 16), :], extra.at[pl.ds(16 * k, 16), :],
                cot_send.at[k, 1], cot_recv.at[k, 1], away[side],
            ),
        ]

    loads[0].wait()
    loads[1].wait()
    pl.semaphore_wait(barrier, len(others) + 2)
    for side in (0, 1):
        start(raw_copy(side, 1))

    loads[2].wait()
    loads[3].wait()
    routes = routes_v[...]
    experts = (lax.broadcasted_iota(jnp.int32, (E, toks), 0) + me) % E
    first_hit = routes[0:1, :] == experts
    second_hit = routes[1:2, :] == experts
    named = jnp.where(first_hit | second_hit, 1.0, 0.0)
    earlier = jnp.where(
        lax.broadcasted_iota(jnp.int32, (toks, toks), 0) < lax.broadcasted_iota(jnp.int32, (toks, toks), 1), 1.0, 0.0
    ).astype(bf16)
    slot_all = jnp.where(named > 0.5, dot(named.astype(bf16), earlier), -1.0)
    gate_all = jnp.where(first_hit, gates_v[0:1, :], 0.0) + jnp.where(second_hit, gates_v[1:2, :], 0.0)
    metas[0, 0:E, :] = slot_all
    metas[0, E:2 * E, :] = gate_all
    for side in (0, 1):
        start(meta_copy(side, 1))

    main_iota = lax.broadcasted_iota(jnp.int32, (MAIN, toks), 0).astype(f32)
    tail_row = lax.broadcasted_iota(jnp.int32, (16, toks), 0)
    tail_iota = (MAIN + tail_row % 2).astype(f32)
    tail_block = tail_row // 2

    def hot(slot):
        return jnp.where(main_iota == slot, 1.0, 0.0)

    def tail_hot(slot, k):
        return jnp.where((tail_iota == slot) & (tail_block == k), 1.0, 0.0)

    slot = slot_all[0:1, :]
    pick = hot(slot)
    loads[4].wait()
    packed = jnp.zeros((16, piece), f32)
    for j in range(E):
        chosen = jnp.concatenate([pick, tail_hot(slot, j)], axis=0).astype(bf16)
        got = dot(chosen, cotangents_v[:, j * piece:(j + 1) * piece])
        rows[2, 0:MAIN, j * piece:(j + 1) * piece] = got[0:MAIN].astype(bf16)
        packed = packed + got[MAIN:]
    extra[0:16, :] = packed.astype(bf16)

    chosen = jnp.concatenate([tail_hot(slot_all[i:i + 1, :], 0) for i in range(E)], axis=0).astype(bf16)
    for a in range(2):
        got = dot(chosen, raw_own[a])
        for i in range(E):
            tails[i, a] = got[i * 16:(i + 1) * 16]

    def pick_copy(side, d, i):
        k = block_of(side, d, i)
        b = side * 4 + d - 1
        return remote(
            stage.at[b, i], rows.at[pl.ds(0, 2), main_rows(k), cols(me)],
            pick_send.at[b, i], pick_recv.at[k, i], others[i - 1],
        )

    def pick_arrived(k):
        for i in range(1, E):
            remote(
                stage.at[0, i], rows.at[pl.ds(0, 2), main_rows(k), cols((me - i + E) % E)],
                pick_send.at[0, i], pick_recv.at[k, i], others[i - 1],
            ).wait_recv()

    def pick_rows(side, d):
        b = side * 4 + d - 1
        live = [i for i in range(E) if block_of(side, d, i) is not None]
        slots_of = [metas[b + 1, i:i + 1, :] for i in live]
        chosen = jnp.concatenate(
            [hot(s) for s in slots_of] + [tail_hot(s, block_of(side, d, i)) for i, s in zip(live, slots_of)], axis=0
        ).astype(bf16)
        for a in range(2):
            got = dot(chosen, raw[b, a])
            for n, i in enumerate(live):
                value = got[n * MAIN:(n + 1) * MAIN].astype(bf16)
                if i == 0:
                    rows[a, main_rows(block_of(side, d, 0)), cols(me)] = value
                else:
                    stage[b, i, a] = value
                first = len(live) * MAIN + n * 16
                tails[i, a] = tails[i, a] + got[first:first + 16]
        for i in live:
            if i:
                start(pick_copy(side, d, i))

    for d in (1, 2, 3, 4):
        for side in (0, 1):
            raw_copy(side, d).wait_recv()
            if d < 4:
                start(raw_copy(side, d + 1))
            meta_copy(side, d).wait_recv()
            if d < 4:
                start(meta_copy(side, d + 1))
        for side in (0, 1):
            if d > 1 and (side == 0 or d <= 4):
                for copy in cot_copies(side, d - 1):
                    copy.wait_recv()
            if side == 0 or d < 4:
                for copy in cot_copies(side, d):
                    start(copy)
        if d == 1:
            loads[5].wait()
            loads[6].wait()
            for a, source in enumerate((acts_v, tangents_v)):
                rows[a, 0:MAIN, :] = dot(pick.astype(bf16), source[...]).astype(bf16)
        for side in (0, 1):
            pick_rows(side, d)

    def tail_copy(i):
        return remote(
            tails_out.at[i], rows.at[pl.ds(0, 2), pl.ds(EXTRA, 16), cols(me)],
            tail_send.at[i], tail_recv.at[i], others[i - 1],
        )

    for i in range(E):
        if i:
            tails_out[i] = tails[i].astype(bf16)
            start(tail_copy(i))
        else:
            rows[0:2, EXTRA:TOTAL, cols(me)] = tails[0].astype(bf16)

    tail_gate = jnp.zeros((16, 1), f32)
    for k in range(N):
        slot_k, gate_k = metas[k, 0:1, :], metas[k, E:E + 1, :]
        gate_rows[main_rows(k), :] = jnp.sum(hot(slot_k) * gate_k, axis=1, keepdims=True)
        tail_gate = tail_gate + jnp.sum(tail_hot(slot_k, k) * gate_k, axis=1, keepdims=True)
    gate_rows[EXTRA:TOTAL, :] = tail_gate

    def compute(first_row, size):
        here = slice(first_row, first_row + size)

        def hidden_tile(n, carry):
            f = pl.ds(pl.multiple_of(n * 256, 256), 256)
            both = dot(rows[0:2, here, :].reshape(2 * size, width), w_in[:, f])
            h, u = both[0:size], both[size:2 * size]
            p = dot(rows[2, here, :], w_out[f, :], NT)
            s = jax.nn.sigmoid(h)
            gate = gate_rows[here, :]
            mid[0, here, f] = (s * (1.0 + h * (1.0 - s)) * u * gate).astype(bf16)
            mid[1, here, f] = (s * (1.0 - s) * (2.0 + h * (1.0 - 2.0 * s)) * u * p * gate).astype(bf16)
            return carry

        lax.fori_loop(0, w_in.shape[1] // 256, hidden_tile, 0)

        def out_tile(n, carry):
            d = pl.ds(pl.multiple_of(n * 256, 256), 256)
            part[0, here, d] = dot(mid[0, here, :], w_out[:, d]).astype(bf16)
            part[1, here, d] = dot(mid[1, here, :], w_in[d, :], NT).astype(bf16)
            return carry

        lax.fori_loop(0, width // 256, out_tile, 0)

    loads[7].wait()
    loads[8].wait()
    for k in (1, 2, 5, 6):
        pick_arrived(k)
    compute(0, EARLY)
    for k in (3, 7, 4):
        pick_arrived(k)
    for i in range(1, E):
        remote(
            tails_out.at[i], rows.at[pl.ds(0, 2), pl.ds(EXTRA, 16), cols((me - i + E) % E)],
            tail_send.at[i], tail_recv.at[i], others[i - 1],
        ).wait_recv()
    for copy in cot_copies(0, 4):
        copy.wait_recv()

    at_row = lax.broadcasted_iota(jnp.int32, (128, 128), 0)
    at_col = lax.broadcasted_iota(jnp.int32, (128, 128), 1)
    turn = (at_row // 16) == (at_col % 16) // 2
    turn = turn & ((at_row % 16) // 2 == at_col // 16) & (at_row % 2 == at_col % 2)
    turn = jnp.where(turn, 1.0, 0.0).astype(bf16)
    turned = dot(turn, extra[...]).astype(bf16)
    for j in range(E):
        rows[2, EXTRA:TOTAL, j * piece:(j + 1) * piece] = turned[j * 16:(j + 1) * 16]
    compute(EARLY, TOTAL - EARLY)

    halves = ((EARLY, TOTAL - EARLY), (0, EARLY))

    def land_copy(half, i):
        r = pl.ds(*halves[half])
        return remote(
            part.at[1, r, cols(others[i - 1][2])], land.at[i, r, :],
            land_send.at[half, i], land_recv.at[half, i], others[i - 1],
        )

    landing = {4: 3, 3: 2, 2: 1, 1: 0, 7: 5, 6: 4, 5: 6}

    def tan_copy(k, c):
        n = landing[k]
        device = behind if k <= 4 else ahead
        if c == 0:
            src, dst = part.at[0, main_rows(k), :], back.at[n]
        else:
            src, dst = part_extra.at[pl.ds(16 * k, 16), :], back_extra.at[n]
        return remote(src, dst, tan_send.at[n, c], tan_recv.at[n, c], device)

    def tan_add(k, k_from):
        n = landing[k_from]
        r, x = main_rows(k), pl.ds(16 * k, 16)
        tan_copy(k_from, 0).wait_recv()
        part[0, r, :] = (part[0, r, :].astype(f32) + back[n].astype(f32)).astype(bf16)
        start(tan_copy(k, 0))
        tan_copy(k_from, 1).wait_recv()
        part_extra[x, :] = (part_extra[x, :].astype(f32) + back_extra[n].astype(f32)).astype(bf16)
        start(tan_copy(k, 1))

    for i in range(1, E):
        start(land_copy(0, i))
    start(tan_copy(4, 0))
    start(tan_copy(7, 0))
    spread = jnp.concatenate([part[0, EXTRA:TOTAL, j * piece:(j + 1) * piece] for j in range(E)], axis=0)
    part_extra[...] = dot(turn, spread).astype(bf16)
    start(tan_copy(4, 1))
    start(tan_copy(7, 1))
    for i in range(1, E):
        start(land_copy(1, i))
    land[0] = part[1, :, cols(me)]

    def combine(side, d):
        b = 0 if d == 0 else side * 4 + d
        chosen, values = [], []
        for i in range(E):
            k = 0 if d == 0 else block_of(side, d, i)
            if k is None:
                continue
            s = metas[b, (E - i) % E:(E - i) % E + 1, :]
            chosen += [hot(s), tail_hot(s, k)]
            values += [land[i, main_rows(k), :], land[i, EXTRA:TOTAL, :]]
        return dot(jnp.concatenate(chosen, axis=0).astype(bf16), jnp.concatenate(values, axis=0), TN)

    def sum_copy(side, d):
        n = side * 4 + d - 1
        return remote(sums.at[n], sums_in.at[n], sum_send.at[n], sum_recv.at[n], home[side])

    def sum_step(side, d):
        value = combine(side, d)
        if d < 4:
            sum_copy(side, d + 1).wait_recv()
            value = value + sums_in[side * 4 + d].astype(f32)
        sums[side * 4 + d - 1] = value.astype(bf16)
        start(sum_copy(side, d))

    tan_add(3, 4)
    tan_add(6, 7)
    for i in range(1, E):
        land_copy(0, i).wait_recv()
    sum_step(0, 4)
    sum_step(1, 4)
    tan_add(2, 3)
    tan_add(5, 6)
    sum_step(0, 3)
    sum_step(1, 3)
    tan_add(1, 2)
    for i in range(1, E):
        land_copy(1, i).wait_recv()
    sum_step(0, 2)
    sum_step(1, 2)

    for c in (0, 1):
        tan_copy(5, c).wait_recv()
        tan_copy(1, c).wait_recv()
    n, m = landing[5], landing[1]
    slots[0:MAIN, :] = (part[0, 0:MAIN, :].astype(f32) + back[n].astype(f32) + back[m].astype(f32)).astype(bf16)
    total = part_extra[0:16, :].astype(f32) + back_extra[n].astype(f32) + back_extra[m].astype(f32)
    total = total.astype(bf16)
    pick_row = lax.broadcasted_iota(jnp.int32, (128, 16), 0)
    pick_col = lax.broadcasted_iota(jnp.int32, (128, 16), 1)
    select = (pick_col == 2 * (pick_row // 16) + pick_row % 16) & (pick_row % 16 < 2)
    unpacked = dot(jnp.where(select, 1.0, 0.0).astype(bf16), total).astype(bf16)
    for j in range(E):
        slots[MAIN:48, j * piece:(j + 1) * piece] = unpacked[j * 16:(j + 1) * 16]

    def swap_copy(i):
        return remote(
            slots.at[:, cols(others[i - 1][2])], final.at[i], swap_send.at[i], swap_recv.at[i], others[i - 1]
        )

    for i in range(1, E):
        start(swap_copy(i))
    final[0] = slots[:, cols(me)]
    sum_step(0, 1)
    sum_step(1, 1)
    own = combine(0, 0)

    slot_iota = lax.broadcasted_iota(jnp.int32, (48, toks), 0).astype(f32)
    spread = jnp.concatenate(
        [jnp.where(slot_iota == metas[0, (E - i) % E:(E - i) % E + 1, :], 1.0, 0.0) for i in range(E)], axis=0
    ).astype(bf16)
    for i in range(1, E):
        swap_copy(i).wait_recv()
    tan_ref[...] = dot(spread, final[...].reshape(E * 48, piece), TN).astype(bf16)
    sum_copy(0, 1).wait_recv()
    sum_copy(1, 1).wait_recv()
    grad_ref[...] = (own + sums_in[0].astype(f32) + sums_in[4].astype(f32)).astype(bf16)
    for copy in sent:
        copy.wait_send()


def solution(mesh):
    runs = Z_RUNS if mesh.shape["dp"] % Z_RUNS == 0 else 1

    def shards(acts, tangents, cotangents, routes, gates, w_in, w_out):
        toks, width = acts.shape
        hidden = w_in.shape[2]
        piece = width // E
        vmem = pl.BlockSpec(memory_space=pltpu.VMEM)
        hbm = pl.BlockSpec(memory_space=pl.ANY)
        bf16, f32 = jnp.bfloat16, jnp.float32

        def sems(*shape):
            return [pltpu.SemaphoreType.DMA(shape)] * 2

        return pl.pallas_call(
            functools.partial(kernel, runs),
            out_shape=[jax.ShapeDtypeStruct((toks, piece), bf16)] * 2,
            in_specs=[hbm] * 7,
            out_specs=[vmem] * 2,
            scratch_shapes=[
                pltpu.VMEM((2, toks), jnp.int32),
                pltpu.VMEM((2, toks), f32),
                pltpu.VMEM((toks, width), bf16),
                pltpu.VMEM((toks, width), bf16),
                pltpu.VMEM((toks, width), bf16),
                pltpu.VMEM((width, hidden), bf16),
                pltpu.VMEM((hidden, width), bf16),
                pltpu.VMEM((2, toks, piece), bf16),
                pltpu.VMEM((8, 2, toks, piece), bf16),
                pltpu.VMEM((9, 2 * E, toks), f32),
                pltpu.VMEM((8, E, 2, MAIN, piece), bf16),
                pltpu.VMEM((E, 2, 16, piece), f32),
                pltpu.VMEM((E, 2, 16, piece), bf16),
                pltpu.VMEM((3, TOTAL, width), bf16),
                pltpu.VMEM((N * 16, piece), bf16),
                pltpu.VMEM((TOTAL, 1), f32),
                pltpu.VMEM((2, TOTAL, hidden), bf16),
                pltpu.VMEM((2, TOTAL, width), bf16),
                pltpu.VMEM((N * 16, piece), bf16),
                pltpu.VMEM((7, MAIN, width), bf16),
                pltpu.VMEM((7, 16, piece), bf16),
                pltpu.VMEM((E, TOTAL, piece), bf16),
                pltpu.VMEM((8, toks, piece), bf16),
                pltpu.VMEM((8, toks, piece), bf16),
                pltpu.VMEM((48, width), bf16),
                pltpu.VMEM((E, 48, piece), bf16),
                pltpu.SemaphoreType.DMA((9,)),
            ]
            + sems(8) + sems(8) + sems(8, 2) + sems(8, 8) + sems(8) + sems(2, 8) + sems(7, 2) + sems(8) + sems(8),
            compiler_params=pltpu.CompilerParams(
                collective_id=0, has_side_effects=True, vmem_limit_bytes=60 * 1024 * 1024
            ),
            cost_estimate=pl.CostEstimate(
                flops=10 * TOTAL * width * hidden, bytes_accessed=4 * width * hidden, transcendentals=TOTAL * hidden
            ),
        )(routes.T, gates.T, acts, tangents, cotangents, w_in, w_out)

    return jax.shard_map(
        shards,
        mesh=mesh,
        in_specs=(
            P(("dp", "seq"), None),
            P(("dp", "seq"), None),
            P(("dp", "seq"), None),
            P(("dp", "seq"), None),
            P(("dp", "seq"), None),
            P("expert", None, "seq"),
            P("expert", "seq", None),
        ),
        out_specs=(P(("dp", "seq"), "expert"), P(("dp", "seq"), "expert")),
        check_vma=False,
    )
```

```python
import functools

import jax
import jax.numpy as jnp
from jax import lax
from jax.experimental import pallas as pl
from jax.experimental.pallas import tpu as pltpu
from jax.sharding import PartitionSpec as P

MESH = pl.DeviceIdType.MESH
E = 8
N = 8
MAIN = 32
Z_RUNS = 4
POS = {0: 0, 1: 1, 2: 2, 5: 3, 6: 4, 3: 5, 7: 6, 4: 7}
EARLY = 5 * MAIN
EXTRA = N * MAIN
TOTAL = EXTRA + 16


def dot(a, b, dims=((1,), (0,))):
    return lax.dot_general(a, b, (dims, ((), ())), preferred_element_type=jnp.float32)


NT = ((1,), (1,))
TN = ((0,), (0,))


def main_rows(k):
    return pl.ds(POS[k] * MAIN, MAIN)


def block_of(side, d, i):
    if (side == 0) == (i % 2 == 0):
        return d
    return 4 + d if d <= 3 else None


def kernel(
    runs, routes_hbm, gates_hbm, acts_hbm, tangents_hbm, cotangents_hbm, w_in_hbm, w_out_hbm,
    tan_ref, grad_ref,
    routes_v, gates_v, acts_v, tangents_v, cotangents_v, w_in, w_out, raw_own, raw, metas, stage, tails, tails_out,
    rows, extra, gate_rows, mid, part, part_extra, back, back_extra, land, sums, sums_in, slots, final,
    load_sems, raw_send, raw_recv, meta_send, meta_recv, cot_send, cot_recv, pick_send, pick_recv,
    tail_send, tail_recv, land_send, land_recv, tan_send, tan_recv, sum_send, sum_recv, swap_send, swap_recv,
):
    dp = lax.axis_index("dp")
    seq = lax.axis_index("seq")
    me = lax.axis_index("expert")
    toks, width = acts_hbm.shape
    piece = width // E
    bf16, f32 = jnp.bfloat16, jnp.float32

    def cols(owner):
        return pl.ds(pl.multiple_of(owner * piece, 128), piece)

    loads = [
        pltpu.make_async_copy(src, dst, load_sems.at[n])
        for n, (src, dst) in enumerate((
            (acts_hbm.at[:, cols(me)], raw_own.at[0]),
            (tangents_hbm.at[:, cols(me)], raw_own.at[1]),
            (routes_hbm, routes_v),
            (gates_hbm, gates_v),
            (cotangents_hbm, cotangents_v),
            (acts_hbm, acts_v),
            (tangents_hbm, tangents_v),
            (w_in_hbm.at[0], w_in),
            (w_out_hbm.at[0], w_out),
        ))
    ]
    for load in loads[:5]:
        load.start()

    ring = runs * N
    place = (dp % runs) * N + seq
    column = dp - dp % runs
    step = 1 - 2 * (me % 2)

    def at(offset):
        there = (place + offset * step + ring) % ring
        return (column + there // N, there % N, me)

    ahead, behind = at(1), at(-1)
    away = (ahead, behind)
    home = (behind, ahead)
    others = [(dp, seq, (me + i) % E) for i in range(1, E)]

    barrier = pltpu.get_barrier_semaphore()
    for device in [ahead, behind] + others:
        pl.semaphore_signal(barrier, inc=1, device_id=device, device_id_type=MESH)

    sent = []

    def remote(src, dst, send, recv, device):
        return pltpu.make_async_remote_copy(
            src_ref=src, dst_ref=dst, send_sem=send, recv_sem=recv, device_id=device, device_id_type=MESH
        )

    def start(copy):
        copy.start()
        sent.append(copy)

    def raw_copy(side, d):
        src = raw_own if d == 1 else raw.at[side * 4 + d - 2]
        n = side * 4 + d - 1
        return remote(src, raw.at[n], raw_send.at[n], raw_recv.at[n], away[side])

    def meta_copy(side, d):
        n = side * 4 + d
        return remote(
            metas.at[0 if d == 1 else n - 1], metas.at[n], meta_send.at[n - 1], meta_recv.at[n - 1], away[side]
        )

    def cot_copies(side, d):
        k = side * 4 + d
        k_from = 0 if d == 1 else k - 1
        return [
            remote(
                rows.at[2, main_rows(k_from), :], rows.at[2, main_rows(k), :],
                cot_send.at[k, 0], cot_recv.at[k, 0], away[side],
            ),
            remote(
                extra.at[pl.ds(16 * k_from, 16), :], extra.at[pl.ds(16 * k, 16), :],
                cot_send.at[k, 1], cot_recv.at[k, 1], away[side],
            ),
        ]

    loads[0].wait()
    loads[1].wait()
    pl.semaphore_wait(barrier, len(others) + 2)
    for side in (0, 1):
        start(raw_copy(side, 1))
    loads[5].start()
    loads[6].start()

    loads[2].wait()
    loads[3].wait()
    routes = routes_v[...]
    experts = (lax.broadcasted_iota(jnp.int32, (E, toks), 0) + me) % E
    first_hit = routes[0:1, :] == experts
    second_hit = routes[1:2, :] == experts
    named = jnp.where(first_hit | second_hit, 1.0, 0.0)
    earlier = jnp.where(
        lax.broadcasted_iota(jnp.int32, (toks, toks), 0) < lax.broadcasted_iota(jnp.int32, (toks, toks), 1), 1.0, 0.0
    ).astype(bf16)
    slot_all = jnp.where(named > 0.5, dot(named.astype(bf16), earlier), -1.0)
    gate_all = jnp.where(first_hit, gates_v[0:1, :], 0.0) + jnp.where(second_hit, gates_v[1:2, :], 0.0)
    metas[0, 0:E, :] = slot_all
    metas[0, E:2 * E, :] = gate_all
    for side in (0, 1):
        start(meta_copy(side, 1))

    main_iota = lax.broadcasted_iota(jnp.int32, (MAIN, toks), 0).astype(f32)
    tail_row = lax.broadcasted_iota(jnp.int32, (16, toks), 0)
    tail_iota = (MAIN + tail_row % 2).astype(f32)
    tail_block = tail_row // 2

    def hot(slot):
        return jnp.where(main_iota == slot, 1.0, 0.0)

    def tail_hot(slot, k):
        return jnp.where((tail_iota == slot) & (tail_block == k), 1.0, 0.0)

    slot = slot_all[0:1, :]
    pick = hot(slot)
    loads[4].wait()
    packed = jnp.zeros((16, piece), f32)
    for j in range(E):
        chosen = jnp.concatenate([pick, tail_hot(slot, j)], axis=0).astype(bf16)
        got = dot(chosen, cotangents_v[:, j * piece:(j + 1) * piece])
        rows[2, 0:MAIN, j * piece:(j + 1) * piece] = got[0:MAIN].astype(bf16)
        packed = packed + got[MAIN:]
    extra[0:16, :] = packed.astype(bf16)

    chosen = jnp.concatenate([tail_hot(slot_all[i:i + 1, :], 0) for i in range(E)], axis=0).astype(bf16)
    for a in range(2):
        got = dot(chosen, raw_own[a])
        for i in range(E):
            tails[i, a] = got[i * 16:(i + 1) * 16]

    def pick_copy(side, d, i):
        k = block_of(side, d, i)
        b = side * 4 + d - 1
        return remote(
            stage.at[b, i], rows.at[pl.ds(0, 2), main_rows(k), cols(me)],
            pick_send.at[b, i], pick_recv.at[k, i], others[i - 1],
        )

    def pick_arrived(k):
        for i in range(1, E):
            remote(
                stage.at[0, i], rows.at[pl.ds(0, 2), main_rows(k), cols((me - i + E) % E)],
                pick_send.at[0, i], pick_recv.at[k, i], others[i - 1],
            ).wait_recv()

    def pick_rows(side, d):
        b = side * 4 + d - 1
        live = [i for i in range(E) if block_of(side, d, i) is not None]
        slots_of = [metas[b + 1, i:i + 1, :] for i in live]
        chosen = jnp.concatenate(
            [hot(s) for s in slots_of] + [tail_hot(s, block_of(side, d, i)) for i, s in zip(live, slots_of)], axis=0
        ).astype(bf16)
        for a in range(2):
            got = dot(chosen, raw[b, a])
            for n, i in enumerate(live):
                value = got[n * MAIN:(n + 1) * MAIN].astype(bf16)
                if i == 0:
                    rows[a, main_rows(block_of(side, d, 0)), cols(me)] = value
                else:
                    stage[b, i, a] = value
                first = len(live) * MAIN + n * 16
                tails[i, a] = tails[i, a] + got[first:first + 16]
        for i in live:
            if i:
                start(pick_copy(side, d, i))

    for d in (1, 2, 3, 4):
        for side in (0, 1):
            raw_copy(side, d).wait_recv()
            if d < 4:
                start(raw_copy(side, d + 1))
            meta_copy(side, d).wait_recv()
            if d < 4:
                start(meta_copy(side, d + 1))
        for side in (0, 1):
            if d > 1 and (side == 0 or d <= 4):
                for copy in cot_copies(side, d - 1):
                    copy.wait_recv()
            if side == 0 or d < 4:
                for copy in cot_copies(side, d):
                    start(copy)
        if d == 1:
            loads[7].start()
            loads[8].start()
            loads[5].wait()
            loads[6].wait()
            for a, source in enumerate((acts_v, tangents_v)):
                rows[a, 0:MAIN, :] = dot(pick.astype(bf16), source[...]).astype(bf16)
        for side in (0, 1):
            pick_rows(side, d)

    def tail_copy(i):
        return remote(
            tails_out.at[i], rows.at[pl.ds(0, 2), pl.ds(EXTRA, 16), cols(me)],
            tail_send.at[i], tail_recv.at[i], others[i - 1],
        )

    for i in range(E):
        if i:
            tails_out[i] = tails[i].astype(bf16)
            start(tail_copy(i))
        else:
            rows[0:2, EXTRA:TOTAL, cols(me)] = tails[0].astype(bf16)

    tail_gate = jnp.zeros((16, 1), f32)
    for k in range(N):
        slot_k, gate_k = metas[k, 0:1, :], metas[k, E:E + 1, :]
        gate_rows[main_rows(k), :] = jnp.sum(hot(slot_k) * gate_k, axis=1, keepdims=True)
        tail_gate = tail_gate + jnp.sum(tail_hot(slot_k, k) * gate_k, axis=1, keepdims=True)
    gate_rows[EXTRA:TOTAL, :] = tail_gate

    def compute(first_row, size):
        here = slice(first_row, first_row + size)

        def hidden_tile(n, carry):
            f = pl.ds(pl.multiple_of(n * 256, 256), 256)
            both = dot(rows[0:2, here, :].reshape(2 * size, width), w_in[:, f])
            h, u = both[0:size], both[size:2 * size]
            p = dot(rows[2, here, :], w_out[f, :], NT)
            s = jax.nn.sigmoid(h)
            gate = gate_rows[here, :]
            mid[0, here, f] = (s * (1.0 + h * (1.0 - s)) * u * gate).astype(bf16)
            mid[1, here, f] = (s * (1.0 - s) * (2.0 + h * (1.0 - 2.0 * s)) * u * p * gate).astype(bf16)
            return carry

        lax.fori_loop(0, w_in.shape[1] // 256, hidden_tile, 0)

        def out_tile(n, carry):
            d = pl.ds(pl.multiple_of(n * 256, 256), 256)
            part[0, here, d] = dot(mid[0, here, :], w_out[:, d]).astype(bf16)
            part[1, here, d] = dot(mid[1, here, :], w_in[d, :], NT).astype(bf16)
            return carry

        lax.fori_loop(0, width // 256, out_tile, 0)

    loads[7].wait()
    loads[8].wait()
    for k in (1, 2, 5, 6):
        pick_arrived(k)
    compute(0, EARLY)
    for k in (3, 7, 4):
        pick_arrived(k)
    for i in range(1, E):
        remote(
            tails_out.at[i], rows.at[pl.ds(0, 2), pl.ds(EXTRA, 16), cols((me - i + E) % E)],
            tail_send.at[i], tail_recv.at[i], others[i - 1],
        ).wait_recv()
    for copy in cot_copies(0, 4):
        copy.wait_recv()

    at_row = lax.broadcasted_iota(jnp.int32, (128, 128), 0)
    at_col = lax.broadcasted_iota(jnp.int32, (128, 128), 1)
    turn = (at_row // 16) == (at_col % 16) // 2
    turn = turn & ((at_row % 16) // 2 == at_col // 16) & (at_row % 2 == at_col % 2)
    turn = jnp.where(turn, 1.0, 0.0).astype(bf16)
    turned = dot(turn, extra[...]).astype(bf16)
    for j in range(E):
        rows[2, EXTRA:TOTAL, j * piece:(j + 1) * piece] = turned[j * 16:(j + 1) * 16]
    compute(EARLY, TOTAL - EARLY)

    halves = ((EARLY, TOTAL - EARLY), (0, EARLY))

    def land_copy(half, i):
        r = pl.ds(*halves[half])
        return remote(
            part.at[1, r, cols(others[i - 1][2])], land.at[i, r, :],
            land_send.at[half, i], land_recv.at[half, i], others[i - 1],
        )

    landing = {4: 3, 3: 2, 2: 1, 1: 0, 7: 5, 6: 4, 5: 6}

    def tan_copy(k, c):
        n = landing[k]
        device = behind if k <= 4 else ahead
        if c == 0:
            src, dst = part.at[0, main_rows(k), :], back.at[n]
        else:
            src, dst = part_extra.at[pl.ds(16 * k, 16), :], back_extra.at[n]
        return remote(src, dst, tan_send.at[n, c], tan_recv.at[n, c], device)

    def tan_add(k, k_from):
        n = landing[k_from]
        r, x = main_rows(k), pl.ds(16 * k, 16)
        tan_copy(k_from, 0).wait_recv()
        part[0, r, :] = (part[0, r, :].astype(f32) + back[n].astype(f32)).astype(bf16)
        start(tan_copy(k, 0))
        tan_copy(k_from, 1).wait_recv()
        part_extra[x, :] = (part_extra[x, :].astype(f32) + back_extra[n].astype(f32)).astype(bf16)
        start(tan_copy(k, 1))

    for i in range(1, E):
        start(land_copy(0, i))
    start(tan_copy(4, 0))
    start(tan_copy(7, 0))
    spread = jnp.concatenate([part[0, EXTRA:TOTAL, j * piece:(j + 1) * piece] for j in range(E)], axis=0)
    part_extra[...] = dot(turn, spread).astype(bf16)
    start(tan_copy(4, 1))
    start(tan_copy(7, 1))
    for i in range(1, E):
        start(land_copy(1, i))
    land[0] = part[1, :, cols(me)]

    def combine(side, d):
        b = 0 if d == 0 else side * 4 + d
        chosen, values = [], []
        for i in range(E):
            k = 0 if d == 0 else block_of(side, d, i)
            if k is None:
                continue
            s = metas[b, (E - i) % E:(E - i) % E + 1, :]
            chosen += [hot(s), tail_hot(s, k)]
            values += [land[i, main_rows(k), :], land[i, EXTRA:TOTAL, :]]
        return dot(jnp.concatenate(chosen, axis=0).astype(bf16), jnp.concatenate(values, axis=0), TN)

    def sum_copy(side, d):
        n = side * 4 + d - 1
        return remote(sums.at[n], sums_in.at[n], sum_send.at[n], sum_recv.at[n], home[side])

    def sum_step(side, d):
        value = combine(side, d)
        if d < 4:
            sum_copy(side, d + 1).wait_recv()
            value = value + sums_in[side * 4 + d].astype(f32)
        sums[side * 4 + d - 1] = value.astype(bf16)
        start(sum_copy(side, d))

    tan_add(3, 4)
    tan_add(6, 7)
    for i in range(1, E):
        land_copy(0, i).wait_recv()
    sum_step(0, 4)
    sum_step(1, 4)
    tan_add(2, 3)
    tan_add(5, 6)
    sum_step(0, 3)
    sum_step(1, 3)
    tan_add(1, 2)
    for i in range(1, E):
        land_copy(1, i).wait_recv()
    sum_step(0, 2)
    sum_step(1, 2)

    for c in (0, 1):
        tan_copy(5, c).wait_recv()
        tan_copy(1, c).wait_recv()
    n, m = landing[5], landing[1]
    slots[0:MAIN, :] = (part[0, 0:MAIN, :].astype(f32) + back[n].astype(f32) + back[m].astype(f32)).astype(bf16)
    total = part_extra[0:16, :].astype(f32) + back_extra[n].astype(f32) + back_extra[m].astype(f32)
    total = total.astype(bf16)
    pick_row = lax.broadcasted_iota(jnp.int32, (128, 16), 0)
    pick_col = lax.broadcasted_iota(jnp.int32, (128, 16), 1)
    select = (pick_col == 2 * (pick_row // 16) + pick_row % 16) & (pick_row % 16 < 2)
    unpacked = dot(jnp.where(select, 1.0, 0.0).astype(bf16), total).astype(bf16)
    for j in range(E):
        slots[MAIN:48, j * piece:(j + 1) * piece] = unpacked[j * 16:(j + 1) * 16]

    def swap_copy(i):
        return remote(
            slots.at[:, cols(others[i - 1][2])], final.at[i], swap_send.at[i], swap_recv.at[i], others[i - 1]
        )

    for i in range(1, E):
        start(swap_copy(i))
    final[0] = slots[:, cols(me)]
    sum_step(0, 1)
    sum_step(1, 1)
    own = combine(0, 0)

    slot_iota = lax.broadcasted_iota(jnp.int32, (48, toks), 0).astype(f32)
    spread = jnp.concatenate(
        [jnp.where(slot_iota == metas[0, (E - i) % E:(E - i) % E + 1, :], 1.0, 0.0) for i in range(E)], axis=0
    ).astype(bf16)
    for i in range(1, E):
        swap_copy(i).wait_recv()
    tan_ref[...] = dot(spread, final[...].reshape(E * 48, piece), TN).astype(bf16)
    sum_copy(0, 1).wait_recv()
    sum_copy(1, 1).wait_recv()
    grad_ref[...] = (own + sums_in[0].astype(f32) + sums_in[4].astype(f32)).astype(bf16)
    for copy in sent:
        copy.wait_send()


def solution(mesh):
    runs = Z_RUNS if mesh.shape["dp"] % Z_RUNS == 0 else 1

    def shards(acts, tangents, cotangents, routes, gates, w_in, w_out):
        toks, width = acts.shape
        hidden = w_in.shape[2]
        piece = width // E
        vmem = pl.BlockSpec(memory_space=pltpu.VMEM)
        hbm = pl.BlockSpec(memory_space=pl.ANY)
        bf16, f32 = jnp.bfloat16, jnp.float32

        def sems(*shape):
            return [pltpu.SemaphoreType.DMA(shape)] * 2

        return pl.pallas_call(
            functools.partial(kernel, runs),
            out_shape=[jax.ShapeDtypeStruct((toks, piece), bf16)] * 2,
            in_specs=[hbm] * 7,
            out_specs=[vmem] * 2,
            scratch_shapes=[
                pltpu.VMEM((2, toks), jnp.int32),
                pltpu.VMEM((2, toks), f32),
                pltpu.VMEM((toks, width), bf16),
                pltpu.VMEM((toks, width), bf16),
                pltpu.VMEM((toks, width), bf16),
                pltpu.VMEM((width, hidden), bf16),
                pltpu.VMEM((hidden, width), bf16),
                pltpu.VMEM((2, toks, piece), bf16),
                pltpu.VMEM((8, 2, toks, piece), bf16),
                pltpu.VMEM((9, 2 * E, toks), f32),
                pltpu.VMEM((8, E, 2, MAIN, piece), bf16),
                pltpu.VMEM((E, 2, 16, piece), f32),
                pltpu.VMEM((E, 2, 16, piece), bf16),
                pltpu.VMEM((3, TOTAL, width), bf16),
                pltpu.VMEM((N * 16, piece), bf16),
                pltpu.VMEM((TOTAL, 1), f32),
                pltpu.VMEM((2, TOTAL, hidden), bf16),
                pltpu.VMEM((2, TOTAL, width), bf16),
                pltpu.VMEM((N * 16, piece), bf16),
                pltpu.VMEM((7, MAIN, width), bf16),
                pltpu.VMEM((7, 16, piece), bf16),
                pltpu.VMEM((E, TOTAL, piece), bf16),
                pltpu.VMEM((8, toks, piece), bf16),
                pltpu.VMEM((8, toks, piece), bf16),
                pltpu.VMEM((48, width), bf16),
                pltpu.VMEM((E, 48, piece), bf16),
                pltpu.SemaphoreType.DMA((9,)),
            ]
            + sems(8) + sems(8) + sems(8, 2) + sems(8, 8) + sems(8) + sems(2, 8) + sems(7, 2) + sems(8) + sems(8),
            compiler_params=pltpu.CompilerParams(
                collective_id=0, has_side_effects=True, vmem_limit_bytes=60 * 1024 * 1024
            ),
            cost_estimate=pl.CostEstimate(
                flops=10 * TOTAL * width * hidden, bytes_accessed=4 * width * hidden, transcendentals=TOTAL * hidden
            ),
        )(routes.T, gates.T, acts, tangents, cotangents, w_in, w_out)

    return jax.shard_map(
        shards,
        mesh=mesh,
        in_specs=(
            P(("dp", "seq"), None),
            P(("dp", "seq"), None),
            P(("dp", "seq"), None),
            P(("dp", "seq"), None),
            P(("dp", "seq"), None),
            P("expert", None, "seq"),
            P("expert", "seq", None),
        ),
        out_specs=(P(("dp", "seq"), "expert"), P(("dp", "seq"), "expert")),
        check_vma=False,
    )
```
